32 devices in a mesh: mp: 8 (over z, y), dp: 4 (over x, core).
Axes of the slice: x: 2, y: 2, z: 4, core: 2. Of those that a mesh axis runs over, the one named last changes fastest.
Arguments:
- momentum: float32 [8192, 28672], P('mp', 'dp'), may hold values from -120 to 120, as said below
- gradient: bfloat16 [8192, 28672], P('mp', 'dp'), may hold values from -4 to 4
- factor_q: bfloat16 [28672, 128], P(('dp', 'mp')), may hold values from -0.03125 to 0.03125
Outputs:
- momentum_out: float32 [8192, 28672], P('mp', 'dp')
- factor_out: bfloat16 [28672, 128], P(('dp', 'mp'))
- update: bfloat16 [8192, 28672], P('mp', 'dp')
The draws below stay inside these ranges and needn't reach their ends.
Inputs may be any that keep to these rules, and one draw needn't show every extreme that they name: `momentum`: entries are finite reals.
All inputs are finite; a program needn't handle non-finite values.
Results may differ from the reference program's by a relative error of at most 0.00135.
Values may be sent and summed in bfloat16 or wider, within the bound.
A program may use at most 192 MiB of HBM per device.

```python
import math
import jax
import jax.numpy as jnp
from jax import lax

D = 8192
FF = 28672
RANK = 128


def draw_momentum(key, part):
    keys = jax.random.split(key, 6)
    row_ramp = 3.0 ** (jnp.arange(D, dtype=jnp.float32) / (D - 1))
    col_ramp = 3.0 ** (jnp.arange(FF, dtype=jnp.float32) / (FF - 1))
    row_scale = 0.5 * row_ramp * jnp.exp(jax.random.uniform(keys[0], (D,), jnp.float32, 0.0, math.log(10.0 / 3.0)))
    col_scale = 0.4 * col_ramp * jnp.exp(jax.random.uniform(keys[1], (FF,), jnp.float32, 0.0, math.log(10.0 / 3.0)))
    base = jax.random.normal(keys[5], (D, FF), jnp.float32)
    base = jnp.clip(base, -6.0, 6.0)
    return (base * row_scale[:, None] * col_scale[None, :]).astype(jnp.float32)


def levels(own_key, shape, cuts, smallest, top_value):
    loudness = 1.0
    for position, blocks in cuts:
        steps = jax.random.uniform(jax.random.fold_in(jax.random.fold_in(own_key, 6), position), (blocks,), jnp.float32, smallest / len(cuts), top_value / len(cuts))
        loudness = loudness * jnp.repeat(jnp.exp(steps), shape[position] // blocks).reshape((-1,) + (1,) * (len(shape) - 1 - position))
    return loudness


def noise(stream_key, extent, scale, limit, pieces=(), kind=jnp.bfloat16):
    gain = levels(stream_key, extent, pieces, -0.22, 0.18) if pieces else 1.0
    drawn = jax.random.normal(stream_key, extent, jnp.float32) * scale * gain
    return jnp.minimum(jnp.maximum(drawn, -limit), limit).astype(kind)


def setup_inputs(seed: int = 0) -> dict:
    splits = jax.random.split(jax.random.key(seed), 4)
    return {
        "momentum": draw_momentum(jax.random.fold_in(splits[3], 71), 0),
        "gradient": noise(splits[1], (D, FF), 0.5, 4.0, ((0, 8), (1, 4))),
        "factor_q": noise(splits[2], (FF, RANK), FF ** -0.5, 0.03125, ((0, 32),)),
    }


highest = lax.Precision.HIGHEST
feedback_rate = 0.05

def reference(momentum, gradient, factor_q):
    blended = momentum + gradient.astype(jnp.float32)
    power_left = jnp.dot(blended, factor_q.astype(jnp.float32), precision=highest)
    gram_matrix = jnp.dot(power_left.T, power_left, precision=highest)
    factor_low = jnp.linalg.cholesky(gram_matrix)
    orthonormal = jax.scipy.linalg.solve_triangular(factor_low, power_left.T, lower=True).T
    power_right = jnp.dot(blended.T, orthonormal, precision=highest)
    column_sums = lax.optimization_barrier(jnp.sum(power_right * power_right, axis=0))
    q_new = power_right * lax.rsqrt(column_sums + 1e-06)
    momentum_out = blended - feedback_rate * jnp.dot(orthonormal, power_right.T, precision=highest)
    scale_factor = math.sqrt(D * FF / RANK)
    update = (scale_factor * jnp.dot(orthonormal, q_new.T, precision=highest)).astype(jnp.bfloat16)
    return (momentum_out, q_new.astype(jnp.bfloat16), update)
```

```python
import functools
import math

import jax
import jax.numpy as jnp
from jax import lax
from jax.experimental import pallas as pl
from jax.experimental.pallas import tpu as pltpu
from jax.sharding import PartitionSpec as P

highest = lax.Precision.HIGHEST
feedback_rate = 0.05
MESH = pl.DeviceIdType.MESH
f32 = jnp.float32
bf16 = jnp.bfloat16


def make_orthonormal(power_left, gram_matrix):
    factor_low = jnp.linalg.cholesky(gram_matrix)
    return jax.scipy.linalg.solve_triangular(factor_low, power_left.T, lower=True).T


def plain(scale_factor, momentum, gradient, factor_q):
    blended = momentum + gradient.astype(f32)
    share_rows = blended.shape[1] // lax.axis_size("mp")
    power_part = jnp.dot(
        blended,
        lax.all_gather(factor_q, "mp", axis=0, tiled=True).astype(f32),
        precision=highest,
    )
    power_left = lax.psum(power_part, "dp")
    gram_matrix = lax.psum(jnp.dot(power_left.T, power_left, precision=highest), "mp")
    orthonormal = make_orthonormal(power_left, gram_matrix)
    right_share = lax.psum_scatter(
        jnp.dot(blended.T, orthonormal, precision=highest), "mp", scatter_dimension=0, tiled=True
    )
    column_sums = lax.psum(jnp.sum(right_share * right_share, axis=0), ("mp", "dp"))
    power_right = lax.all_gather(right_share, "mp", axis=0, tiled=True)
    q_new = power_right * lax.rsqrt(column_sums + 1e-06)
    q_share = lax.dynamic_slice_in_dim(q_new, lax.axis_index("mp") * share_rows, share_rows, 0)
    momentum_out = blended - feedback_rate * jnp.dot(orthonormal, power_right.T, precision=highest)
    update = (scale_factor * jnp.dot(orthonormal, q_new.T, precision=highest)).astype(bf16)
    return (momentum_out, q_share.astype(bf16), update)


def split(value):
    high = value.astype(bf16)
    return high, (value - high.astype(f32)).astype(bf16)


def factors_kernel(n, n_dp, scale_factor, mom_hbm, grad_hbm, q_ref, pr_hbm, o_ref, qout_ref,
                   b_high, b_low, q_all, mom_st, grad_st, part, part_in, left, left_t, left_cat,
                   w, right_in, left_in, gram, gram_in, aug, pr, cs, cs_in, csd_in,
                   load_sem, q_send, q_recv, dp_send, dp_recv, rs_send, rs_recv,
                   gr_send, gr_recv, ag_send, ag_recv, cs_send, cs_recv, out_sem):
    rank = q_ref.shape[1]
    share = q_ref.shape[0]
    rows = mom_hbm.shape[0]
    chunk = rows // n_dp
    half_rows = rows // 2
    half_n = n // 2
    half_rank = rank // 2
    n_bits = n.bit_length() - 1
    me = lax.axis_index("mp")
    my_dp = lax.axis_index("dp")

    def at_place(place):
        back = lax.div(place, half_n)
        return (1 - back) * (2 * place) + back * (2 * (n - 1 - place) + 1)

    odd = lax.rem(me, 2)
    pair = lax.div(me, 2)
    place = (1 - odd) * pair + odd * (n - 1 - pair)

    def owner(offset):
        return at_place(lax.rem(place + (offset + n) % n, n))

    right, left_dev = owner(1), owner(-1)

    def slot(offset):
        offset = (offset + n) % n
        if offset == 0:
            return 0
        if offset == half_n:
            return n - 1
        return 2 * offset if offset < half_n else 2 * (n - offset) - 1

    offsets = [0] * n
    for offset in range(-half_n + 1, half_n + 1):
        offsets[slot(offset)] = offset

    def partner(bit):
        step = 1 << bit
        return me + (1 - 2 * lax.rem(lax.div(me, step), 2)) * step

    def dp_peer(t):
        return lax.rem(my_dp + t, n_dp)

    def remote(src, dst, send, recv, **where):
        return pltpu.make_async_remote_copy(
            src_ref=src, dst_ref=dst, send_sem=send, recv_sem=recv, device_id=where, device_id_type=MESH
        )

    def loads(item):
        block, h = divmod(item, 2)
        cols = pl.ds(pl.multiple_of(owner(offsets[block]) * share, 128), share)
        at = pl.ds(h * half_rows, half_rows)
        return (
            pltpu.make_async_copy(mom_hbm.at[at, cols], mom_st.at[h], load_sem.at[h, 0]),
            pltpu.make_async_copy(grad_hbm.at[at, cols], grad_st.at[h], load_sem.at[h, 1]),
        )

    for item in range(2):
        for copy in loads(item):
            copy.start()

    barrier = pltpu.get_barrier_semaphore()
    greeted = [{"mp": right}, {"mp": left_dev}]
    greeted += [{"mp": partner(bit)} for bit in range(n_bits)]
    greeted += [{"dp": dp_peer(t)} for t in range(1, n_dp)]
    for where in greeted:
        pl.semaphore_signal(barrier, inc=1, device_id=where, device_id_type=MESH)
    pl.semaphore_wait(barrier, len(greeted))

    def gather_copies(s, first, blocks, half, send, recv):
        def at(offset):
            return first if offset == 0 else blocks.at[slot(offset)]

        if s < half_n - 1:
            to_right = (at(-s), blocks.at[slot(-s - 1)])
            to_left = (at(s), blocks.at[slot(s + 1)])
        else:
            low, high = pl.ds(0, half), pl.ds(half, half)
            to_right = (at(-s).at[low], blocks.at[n - 1, low])
            to_left = (at(s).at[high], blocks.at[n - 1, high])
        return (
            remote(*to_right, send.at[s, 0], recv.at[s, 0], mp=right),
            remote(*to_left, send.at[s, 1], recv.at[s, 1], mp=left_dev),
        )

    q_copies = [gather_copies(s, q_ref, q_all, share // 2, q_send, q_recv) for s in range(half_n)]
    for copy in q_copies[0]:
        copy.start()

    part[...] = jnp.zeros_like(part)
    for block in range(n):
        if block % 2 == 1:
            s = block // 2
            for copy in q_copies[s]:
                copy.wait_recv()
            if s + 1 < half_n:
                for copy in q_copies[s + 1]:
                    copy.start()
        q_block = q_ref if block == 0 else q_all.at[block]
        for h in range(2):
            item = 2 * block + h
            for copy in loads(item):
                copy.wait()

            @pl.loop(0, half_rows // chunk if half_rows >= chunk else 1)
            def _(c, block=block, h=h, q_block=q_block):
                size = min(chunk, half_rows)
                at = pl.ds(pl.multiple_of(c * size, 16), size)
                blended = mom_st[h, at, :] + grad_st[h, at, :].astype(f32)
                high, low = split(blended)
                to = pl.ds(pl.multiple_of(h * half_rows + c * size, 16), size)
                b_high[block, to, :] = high
                b_low[block, to, :] = low
                q = q_block[...]
                part[to, :] += jnp.dot(high, q, preferred_element_type=f32) + jnp.dot(
                    low, q, preferred_element_type=f32
                )

            if item + 2 < 2 * n:
                for copy in loads(item + 2):
                    copy.start()

    def rows_of(which):
        return pl.ds(pl.multiple_of(which * chunk, 16), chunk)

    scatter = [
        remote(part.at[rows_of(dp_peer(t))], part_in.at[t - 1], dp_send.at[0, t - 1], dp_recv.at[0, t - 1], dp=dp_peer(t))
        for t in range(1, n_dp)
    ]
    for copy in scatter:
        copy.start()
    for copy in scatter:
        copy.wait_recv()
    total = part[rows_of(my_dp), :]
    for t in range(n_dp - 1):
        total = total + part_in[t]
    left[rows_of(my_dp), :] = total
    handout = [
        remote(left.at[rows_of(my_dp)], left.at[rows_of(my_dp)], dp_send.at[1, t - 1], dp_recv.at[1, t - 1], dp=dp_peer(t))
        for t in range(1, n_dp)
    ]
    for copy in handout:
        copy.start()
    for copy in handout:
        copy.wait_recv()
    transposed = left[...].T
    left_t[...] = transposed
    high, low = split(transposed)
    left_cat[:rank, :] = high
    left_cat[rank:, :] = low

    def make_w(offset):
        k = slot(offset)
        b = b_high[k]
        both = jnp.dot(left_cat[...], b, preferred_element_type=f32)
        w[k] = both[:rank] + both[rank:] + jnp.dot(left_cat[:rank, :], b_low[k], preferred_element_type=f32)

    low_half, high_half = pl.ds(0, half_rank), pl.ds(half_rank, half_rank)

    def ring_copies(s):
        return (
            remote(w.at[slot(-1 - s), low_half], right_in.at[s], rs_send.at[s, 0], rs_recv.at[s, 0], mp=right),
            remote(w.at[slot(1 + s), high_half], left_in.at[s], rs_send.at[s, 1], rs_recv.at[s, 1], mp=left_dev),
        )

    def gram_copy(bit):
        return remote(gram.at[bit], gram_in.at[bit], gr_send.at[bit], gr_recv.at[bit], mp=partner(bit))

    lane = lax.broadcasted_iota(jnp.int32, (rank, rank), 1)
    line = lax.broadcasted_iota(jnp.int32, (rank, rank), 0)

    def eliminate(first, last):
        @pl.loop(first, last)
        def _(k):
            row = aug[pl.ds(k, 1), :]
            column = jnp.sum(jnp.where(lane == k, aug[:, :rank], 0.0), axis=1, keepdims=True)
            pivot = jnp.sum(jnp.where(lane[:1] == k, row[:, :rank], 0.0), axis=1, keepdims=True)
            factor = jnp.where(line[:, :1] > k, column / pivot, 0.0)
            aug[...] = aug[...] - factor * row

    spare = n - 1 - n_bits
    per_step = -(-rank // max(spare, 1))
    made = set()

    def make_once(offset):
        if slot(offset) not in made:
            made.add(slot(offset))
            make_w(offset)

    make_once(-1)
    make_once(1)
    copies = []
    for s in range(n - 1):
        if s > 0:
            before = copies[s - 1]
            before[0].wait_recv()
            k = slot(-1 - s)
            w[k, low_half, :] += right_in[s - 1]
            before[1].wait_recv()
            k = slot(1 + s)
            w[k, high_half, :] += left_in[s - 1]
        copies.append(ring_copies(s))
        for copy in copies[s]:
            copy.start()
        if s == 0:
            gram[0] = jnp.dot(left_t[...], left[...], precision=highest, preferred_element_type=f32)
            gram_copy(0).start()
        elif s <= n_bits:
            gram_copy(s - 1).wait_recv()
            gram[s] = gram[s - 1] + gram_in[s - 1]
            if s < n_bits:
                gram_copy(s).start()
        if s + 1 <= half_n:
            make_once(-2 - s)
            make_once(2 + s)
        if s == half_n - 1 or n == 2:
            make_once(0)
        if s == n_bits:
            aug[:, :rank] = gram[n_bits]
            aug[:, rank:] = jnp.where(lane == line, 1.0, 0.0)
        if s >= n_bits and (s - n_bits) * per_step < rank:
            eliminate((s - n_bits) * per_step, min(rank, (s - n_bits + 1) * per_step))
    diagonal = jnp.sum(jnp.where(lane == line, aug[:, :rank], 0.0), axis=1, keepdims=True)
    inverse_low = aug[:, rank:] / jnp.sqrt(diagonal)

    copies[n - 2][0].wait_recv()
    w[0, low_half, :] += right_in[n - 2]
    copies[n - 2][1].wait_recv()
    w[0, high_half, :] += left_in[n - 2]

    own = jnp.dot(inverse_low, w[0], precision=highest, preferred_element_type=f32)
    pr[0] = own
    ag_copies = [gather_copies(s, pr.at[0], pr, half_rank, ag_send, ag_recv) for s in range(half_n)]
    for copy in ag_copies[0]:
        copy.start()

    def keep(k):
        return pltpu.make_async_copy(pr.at[k], pr_hbm.at[owner(offsets[k])], out_sem.at[k])

    keep(0).start()

    def cs_copy(bit):
        return remote(cs.at[bit], cs_in.at[bit], cs_send.at[bit], cs_recv.at[bit], mp=partner(bit))

    def csd_copy(t):
        return remote(cs.at[n_bits], csd_in.at[t - 1], cs_send.at[n_bits + t - 1], cs_recv.at[n_bits + t - 1], dp=dp_peer(t))

    cs[0] = lax.dot_general(
        jnp.ones((8, share), f32), own * own, (((1,), (1,)), ((), ())), precision=highest, preferred_element_type=f32
    )
    cs_copy(0).start()
    ortho = lax.dot_general(
        left[...], inverse_low, (((1,), (1,)), ((), ())), precision=highest, preferred_element_type=f32
    )
    for bit in range(n_bits):
        cs_copy(bit).wait_recv()
        cs[bit + 1] = cs[bit] + cs_in[bit]
        if bit + 1 < n_bits:
            cs_copy(bit + 1).start()
        if bit < half_n - 1:
            for copy in ag_copies[bit]:
                copy.wait_recv()
            for copy in ag_copies[bit + 1]:
                copy.start()
    for t in range(1, n_dp):
        csd_copy(t).start()
    for s in range(n_bits, half_n - 1):
        for copy in ag_copies[s]:
            copy.wait_recv()
        for copy in ag_copies[s + 1]:
            copy.start()
    for k in range(1, n - 1):
        keep(k).start()
    sums = cs[n_bits]
    for t in range(1, n_dp):
        csd_copy(t).wait_recv()
    for t in range(n_dp - 1):
        sums = sums + csd_in[t]
    scale = 1.0 / jnp.sqrt(sums[:1] + 1e-06)
    o_high, o_low = split(ortho * (scale_factor * scale))
    o_ref[:, :rank] = o_high
    o_ref[:, rank : 2 * rank] = o_low
    o_ref[:, 2 * rank :] = (feedback_rate * ortho).astype(bf16)
    qout_ref[...] = (pr[0].T * scale).astype(bf16)
    for copy in ag_copies[half_n - 1]:
        copy.wait_recv()
    keep(n - 1).start()

    for group in (q_copies, ag_copies, copies):
        for pair_of in group:
            for copy in pair_of:
                copy.wait_send()
    for copy in scatter + handout:
        copy.wait_send()
    for bit in range(n_bits):
        gram_copy(bit).wait_send()
        cs_copy(bit).wait_send()
    for t in range(1, n_dp):
        csd_copy(t).wait_send()
    for k in range(n):
        keep(k).wait()


def outputs_kernel(mom_ref, grad_ref, pr_ref, o_ref, mom_out, update_out):
    rank = pr_ref.shape[1]
    high, low = split(pr_ref[0])
    product = jnp.dot(o_ref[:, : 2 * rank], jnp.concatenate([high, high], axis=0), preferred_element_type=f32)
    product += jnp.dot(o_ref[:, :rank], low, preferred_element_type=f32)
    update_out[...] = product.astype(bf16)
    blended = mom_ref[...] + grad_ref[...].astype(f32)
    mom_out[...] = blended - jnp.dot(o_ref[:, 2 * rank :], high, preferred_element_type=f32)


def fused(n, n_dp, scale_factor, momentum, gradient, factor_q):
    rows, cols = momentum.shape
    share, rank = factor_q.shape
    chunk = rows // n_dp
    n_bits = n.bit_length() - 1
    half_n = n // 2
    dma = pltpu.SemaphoreType.DMA
    vmem = pltpu.VMEM
    whole = pl.BlockSpec(memory_space=pltpu.VMEM)
    anywhere = pl.BlockSpec(memory_space=pl.ANY)
    pr, ortho, q_new = pl.pallas_call(
        functools.partial(factors_kernel, n, n_dp, scale_factor),
        out_shape=(
            jax.ShapeDtypeStruct((n, rank, share), f32),
            jax.ShapeDtypeStruct((rows, 3 * rank), bf16),
            jax.ShapeDtypeStruct((share, rank), bf16),
        ),
        in_specs=[anywhere, anywhere, whole],
        out_specs=(anywhere, whole, whole),
        scratch_shapes=[
            vmem((n, rows, share), bf16),
            vmem((n, rows, share), bf16),
            vmem((n, share, rank), bf16),
            vmem((2, rows // 2, share), f32),
            vmem((2, rows // 2, share), bf16),
            vmem((rows, rank), f32),
            vmem((n_dp - 1, chunk, rank), f32),
            vmem((rows, rank), f32),
            vmem((rank, rows), f32),
            vmem((2 * rank, rows), bf16),
            vmem((n, rank, share), f32),
            vmem((n - 1, rank // 2, share), f32),
            vmem((n - 1, rank // 2, share), f32),
            vmem((n_bits + 1, rank, rank), f32),
            vmem((n_bits, rank, rank), f32),
            vmem((rank, 2 * rank), f32),
            vmem((n, rank, share), f32),
            vmem((n_bits + 1, 8, rank), f32),
            vmem((n_bits, 8, rank), f32),
            vmem((n_dp - 1, 8, rank), f32),
            dma((2, 2)),
            dma((half_n, 2)),
            dma((half_n, 2)),
            dma((2, n_dp - 1)),
            dma((2, n_dp - 1)),
            dma((n - 1, 2)),
            dma((n - 1, 2)),
            dma((n_bits,)),
            dma((n_bits,)),
            dma((half_n, 2)),
            dma((half_n, 2)),
            dma((n_bits + n_dp - 1,)),
            dma((n_bits + n_dp - 1,)),
            dma((n,)),
        ],
        compiler_params=pltpu.CompilerParams(
            collective_id=0, has_side_effects=True, vmem_limit_bytes=60 * 1024 * 1024
        ),
    )(momentum, gradient, factor_q)
    tile = rows // 2
    momentum_out, update = pl.pallas_call(
        outputs_kernel,
        grid=(n, rows // tile),
        out_shape=(
            jax.ShapeDtypeStruct((rows, cols), f32),
            jax.ShapeDtypeStruct((rows, cols), bf16),
        ),
        in_specs=[
            pl.BlockSpec((tile, share), lambda j, i: (i, j)),
            pl.BlockSpec((tile, share), lambda j, i: (i, j)),
            pl.BlockSpec((1, rank, share), lambda j, i: (j, 0, 0)),
            pl.BlockSpec((tile, 3 * rank), lambda j, i: (i, 0)),
        ],
        out_specs=(
            pl.BlockSpec((tile, share), lambda j, i: (i, j)),
            pl.BlockSpec((tile, share), lambda j, i: (i, j)),
        ),
        compiler_params=pltpu.CompilerParams(vmem_limit_bytes=40 * 1024 * 1024),
    )(momentum, gradient, pr, ortho)
    return momentum_out, q_new, update


def solution(mesh):
    n, n_dp = mesh.shape["mp"], mesh.shape["dp"]

    def local(momentum, gradient, factor_q):
        rows, cols = momentum.shape
        share, rank = factor_q.shape
        scale_factor = math.sqrt(rows * n * cols * n_dp / rank)
        tiles = (
            share % 128 == 0
            and rank % 128 == 0
            and rows % (32 * n_dp) == 0
            and n >= 2
            and n & (n - 1) == 0
            and n_dp >= 2
            and 4 * rows * cols <= 32 * 1024 * 1024
        )
        if tiles:
            return fused(n, n_dp, scale_factor, momentum, gradient, factor_q)
        return plain(scale_factor, momentum, gradient, factor_q)

    return jax.shard_map(
        local,
        mesh=mesh,
        in_specs=(P("mp", "dp"), P("mp", "dp"), P(("dp", "mp"), None)),
        out_specs=(P("mp", "dp"), P(("dp", "mp"), None), P("mp", "dp")),
        check_vma=False,
    )
```

```python
import functools
import math

import jax
import jax.numpy as jnp
from jax import lax
from jax.experimental import pallas as pl
from jax.experimental.pallas import tpu as pltpu
from jax.sharding import PartitionSpec as P

highest = lax.Precision.HIGHEST
feedback_rate = 0.05
MESH = pl.DeviceIdType.MESH
f32 = jnp.float32
bf16 = jnp.bfloat16


def make_orthonormal(power_left, gram_matrix):
    factor_low = jnp.linalg.cholesky(gram_matrix)
    return jax.scipy.linalg.solve_triangular(factor_low, power_left.T, lower=True).T


def plain(scale_factor, momentum, gradient, factor_q):
    blended = momentum + gradient.astype(f32)
    share_rows = blended.shape[1] // lax.axis_size("mp")
    power_part = jnp.dot(
        blended,
        lax.all_gather(factor_q, "mp", axis=0, tiled=True).astype(f32),
        precision=highest,
    )
    power_left = lax.psum(power_part, "dp")
    gram_matrix = lax.psum(jnp.dot(power_left.T, power_left, precision=highest), "mp")
    orthonormal = make_orthonormal(power_left, gram_matrix)
    right_share = lax.psum_scatter(
        jnp.dot(blended.T, orthonormal, precision=highest), "mp", scatter_dimension=0, tiled=True
    )
    column_sums = lax.psum(jnp.sum(right_share * right_share, axis=0), ("mp", "dp"))
    power_right = lax.all_gather(right_share, "mp", axis=0, tiled=True)
    q_new = power_right * lax.rsqrt(column_sums + 1e-06)
    q_share = lax.dynamic_slice_in_dim(q_new, lax.axis_index("mp") * share_rows, share_rows, 0)
    momentum_out = blended - feedback_rate * jnp.dot(orthonormal, power_right.T, precision=highest)
    update = (scale_factor * jnp.dot(orthonormal, q_new.T, precision=highest)).astype(bf16)
    return (momentum_out, q_share.astype(bf16), update)


def split(value):
    high = value.astype(bf16)
    return high, (value - high.astype(f32)).astype(bf16)


def factors_kernel(n, n_dp, scale_factor, mom_hbm, grad_hbm, q_ref, pr_own, pr_before, pr_after, o_ref, qout_ref,
                   b_high, b_low, q_all, mom_st, grad_st, part, part_in, left, left_t, left_cat,
                   w, right_in, left_in, gram, gram_in, aug, pr, cs, cs_in, csd_in,
                   load_sem, q_send, q_recv, dp_send, dp_recv, rs_send, rs_recv,
                   gr_send, gr_recv, ag_send, ag_recv, cs_send, cs_recv, out_sem):
    rank = q_ref.shape[1]
    share = q_ref.shape[0]
    rows = mom_hbm.shape[0]
    chunk = rows // n_dp
    half_rows = rows // 2
    half_n = n // 2
    half_rank = rank // 2
    n_bits = n.bit_length() - 1
    me = lax.axis_index("mp")
    my_dp = lax.axis_index("dp")

    def at_place(place):
        back = lax.div(place, half_n)
        return (1 - back) * (2 * place) + back * (2 * (n - 1 - place) + 1)

    odd = lax.rem(me, 2)
    pair = lax.div(me, 2)
    place = (1 - odd) * pair + odd * (n - 1 - pair)

    def owner(offset):
        return at_place(lax.rem(place + (offset + n) % n, n))

    right, left_dev = owner(1), owner(-1)

    def slot(offset):
        offset = (offset + n) % n
        if offset == 0:
            return 0
        if offset == half_n:
            return n - 1
        return 2 * offset if offset < half_n else 2 * (n - offset) - 1

    offsets = [0] * n
    for offset in range(-half_n + 1, half_n + 1):
        offsets[slot(offset)] = offset

    def partner(bit):
        step = 1 << bit
        return me + (1 - 2 * lax.rem(lax.div(me, step), 2)) * step

    def dp_peer(t):
        return lax.rem(my_dp + t, n_dp)

    def remote(src, dst, send, recv, **where):
        return pltpu.make_async_remote_copy(
            src_ref=src, dst_ref=dst, send_sem=send, recv_sem=recv, device_id=where, device_id_type=MESH
        )

    def loads(item):
        block, h = divmod(item, 2)
        cols = pl.ds(pl.multiple_of(owner(offsets[block]) * share, 128), share)
        at = pl.ds(h * half_rows, half_rows)
        return (
            pltpu.make_async_copy(mom_hbm.at[at, cols], mom_st.at[h], load_sem.at[h, 0]),
            pltpu.make_async_copy(grad_hbm.at[at, cols], grad_st.at[h], load_sem.at[h, 1]),
        )

    for item in range(2):
        for copy in loads(item):
            copy.start()

    barrier = pltpu.get_barrier_semaphore()
    greeted = [{"mp": right}, {"mp": left_dev}]
    greeted += [{"mp": partner(bit)} for bit in range(n_bits)]
    greeted += [{"dp": dp_peer(t)} for t in range(1, n_dp)]
    for where in greeted:
        pl.semaphore_signal(barrier, inc=1, device_id=where, device_id_type=MESH)
    pl.semaphore_wait(barrier, len(greeted))

    def gather_copies(s, first, blocks, half, send, recv):
        def at(offset):
            return first if offset == 0 else blocks.at[slot(offset)]

        if s < half_n - 1:
            to_right = (at(-s), blocks.at[slot(-s - 1)])
            to_left = (at(s), blocks.at[slot(s + 1)])
        else:
            low, high = pl.ds(0, half), pl.ds(half, half)
            to_right = (at(-s).at[low], blocks.at[n - 1, low])
            to_left = (at(s).at[high], blocks.at[n - 1, high])
        return (
            remote(*to_right, send.at[s, 0], recv.at[s, 0], mp=right),
            remote(*to_left, send.at[s, 1], recv.at[s, 1], mp=left_dev),
        )

    q_copies = [gather_copies(s, q_ref, q_all, share // 2, q_send, q_recv) for s in range(half_n)]
    for copy in q_copies[0]:
        copy.start()

    part[...] = jnp.zeros_like(part)
    for block in range(n):
        if block % 2 == 1:
            s = block // 2
            for copy in q_copies[s]:
                copy.wait_recv()
            if s + 1 < half_n:
                for copy in q_copies[s + 1]:
                    copy.start()
        q_block = q_ref if block == 0 else q_all.at[block]
        for h in range(2):
            item = 2 * block + h
            for copy in loads(item):
                copy.wait()

            @pl.loop(0, half_rows // chunk if half_rows >= chunk else 1)
            def _(c, block=block, h=h, q_block=q_block):
                size = min(chunk, half_rows)
                at = pl.ds(pl.multiple_of(c * size, 16), size)
                blended = mom_st[h, at, :] + grad_st[h, at, :].astype(f32)
                high, low = split(blended)
                to = pl.ds(pl.multiple_of(h * half_rows + c * size, 16), size)
                b_high[block, to, :] = high
                b_low[block, to, :] = low
                q = q_block[...]
                part[to, :] += jnp.dot(high, q, preferred_element_type=f32) + jnp.dot(
                    low, q, preferred_element_type=f32
                )

            if item + 2 < 2 * n:
                for copy in loads(item + 2):
                    copy.start()

    core = lax.rem(my_dp, 2)
    mate = my_dp + 1 - 2 * core

    def rows_of(which):
        return pl.ds(pl.multiple_of(which * half_rows, 16), half_rows)

    mine = rows_of(core)
    dp_copies = [remote(part.at[rows_of(1 - core)], part_in.at[0], dp_send.at[0], dp_recv.at[0], dp=mate)]
    dp_copies[0].start()
    dp_copies[0].wait_recv()
    part[mine, :] += part_in[0]
    for t in range(1, n_dp // 2):
        copy = remote(part.at[mine], part_in.at[t], dp_send.at[t], dp_recv.at[t], dp=dp_peer(2 * t))
        copy.start()
        dp_copies.append(copy)
    total = part[mine, :]
    for t in range(1, n_dp // 2):
        dp_copies[t].wait_recv()
        total = total + part_in[t]
    left[mine, :] = total
    handout = remote(left.at[mine], left.at[mine], dp_send.at[n_dp // 2], dp_recv.at[n_dp // 2], dp=mate)
    handout.start()
    handout.wait_recv()
    transposed = left[...].T
    left_t[...] = transposed
    high, low = split(transposed)
    left_cat[:rank, :] = high
    left_cat[rank:, :] = low

    def make_w(offset):
        k = slot(offset)
        b = b_high[k]
        both = jnp.dot(left_cat[...], b, preferred_element_type=f32)
        w[k] = both[:rank] + both[rank:] + jnp.dot(left_cat[:rank, :], b_low[k], preferred_element_type=f32)

    low_half, high_half = pl.ds(0, half_rank), pl.ds(half_rank, half_rank)

    def ring_copies(s):
        return (
            remote(w.at[slot(-1 - s), low_half], right_in.at[s], rs_send.at[s, 0], rs_recv.at[s, 0], mp=right),
            remote(w.at[slot(1 + s), high_half], left_in.at[s], rs_send.at[s, 1], rs_recv.at[s, 1], mp=left_dev),
        )

    def gram_copy(bit):
        return remote(gram.at[bit], gram_in.at[bit], gr_send.at[bit], gr_recv.at[bit], mp=partner(bit))

    lane = lax.broadcasted_iota(jnp.int32, (rank, rank), 1)
    line = lax.broadcasted_iota(jnp.int32, (rank, rank), 0)

    def eliminate(first, last):
        @pl.loop(first, last)
        def _(k):
            row = aug[pl.ds(k, 1), :]
            column = jnp.sum(jnp.where(lane == k, aug[:, :rank], 0.0), axis=1, keepdims=True)
            pivot = jnp.sum(jnp.where(lane[:1] == k, row[:, :rank], 0.0), axis=1, keepdims=True)
            factor = jnp.where(line[:, :1] > k, column / pivot, 0.0)
            aug[...] = aug[...] - factor * row

    spare = n - 1 - n_bits
    per_step = -(-rank // max(spare, 1))
    made = set()

    def make_once(offset):
        if slot(offset) not in made:
            made.add(slot(offset))
            make_w(offset)

    make_once(-1)
    make_once(1)
    copies = []
    for s in range(n - 1):
        if s > 0:
            before = copies[s - 1]
            before[0].wait_recv()
            k = slot(-1 - s)
            w[k, low_half, :] += right_in[s - 1]
            before[1].wait_recv()
            k = slot(1 + s)
            w[k, high_half, :] += left_in[s - 1]
        copies.append(ring_copies(s))
        for copy in copies[s]:
            copy.start()
        if s == 0:
            gram[0] = jnp.dot(left_t[...], left[...], precision=highest, preferred_element_type=f32)
            gram_copy(0).start()
        elif s <= n_bits:
            gram_copy(s - 1).wait_recv()
            gram[s] = gram[s - 1] + gram_in[s - 1]
            if s < n_bits:
                gram_copy(s).start()
        if s + 1 <= half_n:
            make_once(-2 - s)
            make_once(2 + s)
        if s == half_n - 1 or n == 2:
            make_once(0)
        if s == n_bits:
            aug[:, :rank] = gram[n_bits]
            aug[:, rank:] = jnp.where(lane == line, 1.0, 0.0)
        if s >= n_bits and (s - n_bits) * per_step < rank:
            eliminate((s - n_bits) * per_step, min(rank, (s - n_bits + 1) * per_step))
    diagonal = jnp.sum(jnp.where(lane == line, aug[:, :rank], 0.0), axis=1, keepdims=True)
    inverse_low = aug[:, rank:] / jnp.sqrt(diagonal)

    copies[n - 2][0].wait_recv()
    w[0, low_half, :] += right_in[n - 2]
    copies[n - 2][1].wait_recv()
    w[0, high_half, :] += left_in[n - 2]

    own = jnp.dot(inverse_low, w[0], precision=highest, preferred_element_type=f32)
    pr[0] = own
    ag_copies = gather_copies(0, pr.at[0], pr, half_rank, ag_send, ag_recv)
    for copy in ag_copies:
        copy.start()

    def keep(k):
        return pltpu.make_async_copy(pr.at[k], (pr_own, pr_before, pr_after)[k], out_sem.at[k])

    keep(0).start()

    def cs_copy(bit):
        return remote(cs.at[bit], cs_in.at[bit], cs_send.at[bit], cs_recv.at[bit], mp=partner(bit))

    def csd_copy(t):
        return remote(cs.at[n_bits], csd_in.at[t - 1], cs_send.at[n_bits + t - 1], cs_recv.at[n_bits + t - 1], dp=dp_peer(t))

    cs[0] = lax.dot_general(
        jnp.ones((8, share), f32), own * own, (((1,), (1,)), ((), ())), precision=highest, preferred_element_type=f32
    )
    cs_copy(0).start()
    ortho = lax.dot_general(
        left[...], inverse_low, (((1,), (1,)), ((), ())), precision=highest, preferred_element_type=f32
    )
    for bit in range(n_bits):
        cs_copy(bit).wait_recv()
        cs[bit + 1] = cs[bit] + cs_in[bit]
        if bit + 1 < n_bits:
            cs_copy(bit + 1).start()
    for t in range(1, n_dp):
        csd_copy(t).start()
    sums = cs[n_bits]
    for t in range(1, n_dp):
        csd_copy(t).wait_recv()
    for t in range(n_dp - 1):
        sums = sums + csd_in[t]
    scale = 1.0 / jnp.sqrt(sums[:1] + 1e-06)
    o_high, o_low = split(ortho * (scale_factor * scale))
    o_ref[:, :rank] = o_high
    o_ref[:, rank : 2 * rank] = o_low
    o_ref[:, 2 * rank :] = (feedback_rate * ortho).astype(bf16)
    qout_ref[...] = (pr[0].T * scale).astype(bf16)
    for copy, k in zip(ag_copies, (1, 2)):
        copy.wait_recv()
        keep(k).start()

    for group in (q_copies, [ag_copies], copies):
        for pair_of in group:
            for copy in pair_of:
                copy.wait_send()
    for copy in dp_copies + [handout]:
        copy.wait_send()
    for bit in range(n_bits):
        gram_copy(bit).wait_send()
        cs_copy(bit).wait_send()
    for t in range(1, n_dp):
        csd_copy(t).wait_send()
    for k in range(3):
        keep(k).wait()


def outputs_kernel(pieces, idx_ref, mom_ref, grad_ref, o_ref, *refs):
    del idx_ref
    block = pl.program_id(0)
    mom_out, update_out = refs[-2:]
    values, first = [], 0
    for count in pieces:
        parts = [ref[...] for ref in refs[first : first + count]]
        values.append(parts[0] if count == 1 else jnp.concatenate(parts, axis=0))
        first += count
    value = values[0]
    for k in range(1, len(values)):
        value = jnp.where(block == k, values[k], value)
    rank = value.shape[0]
    high, low = split(value)
    product = jnp.dot(o_ref[:, : 2 * rank], jnp.concatenate([high, high], axis=0), preferred_element_type=f32)
    product += jnp.dot(o_ref[:, :rank], low, preferred_element_type=f32)
    update_out[...] = product.astype(bf16)
    blended = mom_ref[...] + grad_ref[...].astype(f32)
    mom_out[...] = blended - jnp.dot(o_ref[:, 2 * rank :], high, preferred_element_type=f32)


def write_outputs(blocks, owners, momentum, gradient, ortho, outputs):
    rows, cols = momentum.shape
    pieces = tuple(len(parts) for parts in blocks)
    flat = [part for parts in blocks for part in parts]
    share = flat[0].shape[1]
    rank = ortho.shape[1] // 3
    tile = rows // 4
    def columns():
        return pl.BlockSpec((tile, share), lambda j, i, idx: (i, idx[j]))

    whole = pl.BlockSpec(memory_space=pltpu.VMEM)
    anywhere = pl.BlockSpec(memory_space=pl.ANY)
    given = [] if outputs is None else list(outputs)
    kernel = functools.partial(outputs_kernel, pieces)
    first = 4 + len(flat)
    area = len(blocks) * rows * share
    return pl.pallas_call(
        kernel,
        grid_spec=pltpu.PrefetchScalarGridSpec(
            num_scalar_prefetch=1,
            grid=(len(blocks), rows // tile),
            in_specs=[
                columns(),
                columns(),
                pl.BlockSpec((tile, 3 * rank), lambda j, i, idx: (i, 0)),
                *[whole for _ in flat],
                *[anywhere for _ in given],
            ],
            out_specs=(columns(), columns()),
        ),
        out_shape=(
            jax.ShapeDtypeStruct((rows, cols), f32),
            jax.ShapeDtypeStruct((rows, cols), bf16),
        ),
        input_output_aliases={first: 0, first + 1: 1} if given else {},
        cost_estimate=pl.CostEstimate(flops=8 * rank * area, bytes_accessed=12 * area, transcendentals=0),
        compiler_params=pltpu.CompilerParams(vmem_limit_bytes=60 * 1024 * 1024),
    )(owners, momentum, gradient, ortho, *flat, *given)


def fused(n, n_dp, scale_factor, momentum, gradient, factor_q):
    rows, cols = momentum.shape
    share, rank = factor_q.shape
    n_bits = n.bit_length() - 1
    half_n = n // 2
    dma = pltpu.SemaphoreType.DMA
    vmem = pltpu.VMEM
    whole = pl.BlockSpec(memory_space=pltpu.VMEM)
    anywhere = pl.BlockSpec(memory_space=pl.ANY)
    own, before, after, ortho, q_new = pl.pallas_call(
        functools.partial(factors_kernel, n, n_dp, scale_factor),
        out_shape=(
            *[jax.ShapeDtypeStruct((rank, share), f32)] * 3,
            jax.ShapeDtypeStruct((rows, 3 * rank), bf16),
            jax.ShapeDtypeStruct((share, rank), bf16),
        ),
        in_specs=[anywhere, anywhere, whole],
        out_specs=(anywhere, anywhere, anywhere, whole, whole),
        scratch_shapes=[
            vmem((n, rows, share), bf16),
            vmem((n, rows, share), bf16),
            vmem((n, share, rank), bf16),
            vmem((2, rows // 2, share), f32),
            vmem((2, rows // 2, share), bf16),
            vmem((rows, rank), f32),
            vmem((n_dp // 2, rows // 2, rank), f32),
            vmem((rows, rank), f32),
            vmem((rank, rows), f32),
            vmem((2 * rank, rows), bf16),
            vmem((n, rank, share), f32),
            vmem((n - 1, rank // 2, share), f32),
            vmem((n - 1, rank // 2, share), f32),
            vmem((n_bits + 1, rank, rank), f32),
            vmem((n_bits, rank, rank), f32),
            vmem((rank, 2 * rank), f32),
            vmem((3, rank, share), f32),
            vmem((n_bits + 1, 8, rank), f32),
            vmem((n_bits, 8, rank), f32),
            vmem((n_dp - 1, 8, rank), f32),
            dma((2, 2)),
            dma((half_n, 2)),
            dma((half_n, 2)),
            dma((n_dp // 2 + 1,)),
            dma((n_dp // 2 + 1,)),
            dma((n - 1, 2)),
            dma((n - 1, 2)),
            dma((n_bits,)),
            dma((n_bits,)),
            dma((1, 2)),
            dma((1, 2)),
            dma((n_bits + n_dp - 1,)),
            dma((n_bits + n_dp - 1,)),
            dma((3,)),
        ],
        compiler_params=pltpu.CompilerParams(
            collective_id=0, has_side_effects=True, vmem_limit_bytes=60 * 1024 * 1024
        ),
    )(momentum, gradient, factor_q)

    ring = [2 * p if p < half_n else 2 * (n - 1 - p) + 1 for p in range(n)]
    up = [(ring[p], ring[(p + 1) % n]) for p in range(n)]
    down = [(b, a) for a, b in up]
    me = lax.axis_index("mp")
    odd = lax.rem(me, 2)
    place = (1 - odd) * lax.div(me, 2) + odd * (n - 1 - lax.div(me, 2))

    def owners(*offsets):
        at = lax.rem(place + n + jnp.array(offsets, jnp.int32), jnp.int32(n))
        back = lax.div(at, jnp.int32(half_n))
        return (1 - back) * (2 * at) + back * (2 * (n - 1 - at) + 1)

    outputs = None
    ready, at = [(own,), (before,), (after,)], owners(0, -1, 1)
    for s in range(1, half_n):
        if s < half_n - 1:
            before = lax.ppermute(before, "mp", up)
            after = lax.ppermute(after, "mp", down)
            coming, then = [(before,), (after,)], owners(-1 - s, 1 + s)
        else:
            low = lax.ppermute(before[: rank // 2], "mp", up)
            high = lax.ppermute(after[rank // 2 :], "mp", down)
            coming, then = [(low, high)], owners(half_n)
        outputs = write_outputs(ready, at, momentum, gradient, ortho, outputs)
        outputs, coming = lax.optimization_barrier((outputs, coming))
        if s < half_n - 1:
            (before,), (after,) = coming
        ready, at = coming, then
    momentum_out, update = write_outputs(ready, at, momentum, gradient, ortho, outputs)
    return momentum_out, q_new, update


def solution(mesh):
    n, n_dp = mesh.shape["mp"], mesh.shape["dp"]

    def local(momentum, gradient, factor_q):
        rows, cols = momentum.shape
        share, rank = factor_q.shape
        scale_factor = math.sqrt(rows * n * cols * n_dp / rank)
        tiles = (
            share % 128 == 0
            and rank % 128 == 0
            and rows % (32 * n_dp) == 0
            and n >= 4
            and n & (n - 1) == 0
            and n_dp % 2 == 0
            and 4 * rows * cols <= 32 * 1024 * 1024
        )
        if tiles:
            return fused(n, n_dp, scale_factor, momentum, gradient, factor_q)
        return plain(scale_factor, momentum, gradient, factor_q)

    return jax.shard_map(
        local,
        mesh=mesh,
        in_specs=(P("mp", "dp"), P("mp", "dp"), P(("dp", "mp"), None)),
        out_specs=(P("mp", "dp"), P(("dp", "mp"), None), P("mp", "dp")),
        check_vma=False,
    )
```

```python
import functools
import math

import jax
import jax.numpy as jnp
from jax import lax
from jax.experimental import pallas as pl
from jax.experimental.pallas import tpu as pltpu
from jax.sharding import PartitionSpec as P

highest = lax.Precision.HIGHEST
feedback_rate = 0.05
MESH = pl.DeviceIdType.MESH
f32 = jnp.float32
bf16 = jnp.bfloat16


def make_orthonormal(power_left, gram_matrix):
    factor_low = jnp.linalg.cholesky(gram_matrix)
    return jax.scipy.linalg.solve_triangular(factor_low, power_left.T, lower=True).T


def plain(scale_factor, momentum, gradient, factor_q):
    blended = momentum + gradient.astype(f32)
    share_rows = blended.shape[1] // lax.axis_size("mp")
    power_part = jnp.dot(
        blended,
        lax.all_gather(factor_q, "mp", axis=0, tiled=True).astype(f32),
        precision=highest,
    )
    power_left = lax.psum(power_part, "dp")
    gram_matrix = lax.psum(jnp.dot(power_left.T, power_left, precision=highest), "mp")
    orthonormal = make_orthonormal(power_left, gram_matrix)
    right_share = lax.psum_scatter(
        jnp.dot(blended.T, orthonormal, precision=highest), "mp", scatter_dimension=0, tiled=True
    )
    column_sums = lax.psum(jnp.sum(right_share * right_share, axis=0), ("mp", "dp"))
    power_right = lax.all_gather(right_share, "mp", axis=0, tiled=True)
    q_new = power_right * lax.rsqrt(column_sums + 1e-06)
    q_share = lax.dynamic_slice_in_dim(q_new, lax.axis_index("mp") * share_rows, share_rows, 0)
    momentum_out = blended - feedback_rate * jnp.dot(orthonormal, power_right.T, precision=highest)
    update = (scale_factor * jnp.dot(orthonormal, q_new.T, precision=highest)).astype(bf16)
    return (momentum_out, q_share.astype(bf16), update)


def split(value):
    high = value.astype(bf16)
    return high, (value - high.astype(f32)).astype(bf16)


def factors_kernel(n, n_dp, scale_factor, mom_hbm, grad_hbm, q_ref, pr_own, pr_before, pr_after, o_ref, qout_ref,
                   b_high, b_low, q_all, mom_st, grad_st, part, part_in, left, left_t, left_cat,
                   w, right_in, left_in, gram, gram_in, aug, pr, cs, cs_in, csd_in,
                   load_sem, q_send, q_recv, dp_send, dp_recv, rs_send, rs_recv,
                   gr_send, gr_recv, ag_send, ag_recv, cs_send, cs_recv, out_sem):
    rank = q_ref.shape[1]
    share = q_ref.shape[0]
    rows = mom_hbm.shape[0]
    chunk = rows // n_dp
    half_rows = rows // 2
    half_n = n // 2
    half_rank = rank // 2
    n_bits = n.bit_length() - 1
    me = lax.axis_index("mp")
    my_dp = lax.axis_index("dp")

    def at_place(place):
        back = lax.div(place, half_n)
        return (1 - back) * (2 * place) + back * (2 * (n - 1 - place) + 1)

    odd = lax.rem(me, 2)
    pair = lax.div(me, 2)
    place = (1 - odd) * pair + odd * (n - 1 - pair)

    def owner(offset):
        return at_place(lax.rem(place + (offset + n) % n, n))

    right, left_dev = owner(1), owner(-1)

    def slot(offset):
        offset = (offset + n) % n
        if offset == 0:
            return 0
        if offset == half_n:
            return n - 1
        return 2 * offset if offset < half_n else 2 * (n - offset) - 1

    offsets = [0] * n
    for offset in range(-half_n + 1, half_n + 1):
        offsets[slot(offset)] = offset

    def partner(bit):
        step = 1 << bit
        return me + (1 - 2 * lax.rem(lax.div(me, step), 2)) * step

    def dp_peer(t):
        return lax.rem(my_dp + t, n_dp)

    def remote(src, dst, send, recv, **where):
        return pltpu.make_async_remote_copy(
            src_ref=src, dst_ref=dst, send_sem=send, recv_sem=recv, device_id=where, device_id_type=MESH
        )

    def loads(item):
        block, h = divmod(item, 2)
        cols = pl.ds(pl.multiple_of(owner(offsets[block]) * share, 128), share)
        at = pl.ds(h * half_rows, half_rows)
        return (
            pltpu.make_async_copy(mom_hbm.at[at, cols], mom_st.at[h], load_sem.at[h, 0]),
            pltpu.make_async_copy(grad_hbm.at[at, cols], grad_st.at[h], load_sem.at[h, 1]),
        )

    for item in range(2):
        for copy in loads(item):
            copy.start()

    barrier = pltpu.get_barrier_semaphore()
    greeted = [{"mp": right}, {"mp": left_dev}]
    greeted += [{"mp": partner(bit)} for bit in range(n_bits)]
    greeted += [{"dp": dp_peer(t)} for t in range(1, n_dp)]
    for where in greeted:
        pl.semaphore_signal(barrier, inc=1, device_id=where, device_id_type=MESH)
    pl.semaphore_wait(barrier, len(greeted))

    def gather_copies(s, first, blocks, half, send, recv):
        def at(offset):
            return first if offset == 0 else blocks.at[slot(offset)]

        if s < half_n - 1:
            to_right = (at(-s), blocks.at[slot(-s - 1)])
            to_left = (at(s), blocks.at[slot(s + 1)])
        else:
            low, high = pl.ds(0, half), pl.ds(half, half)
            to_right = (at(-s).at[low], blocks.at[n - 1, low])
            to_left = (at(s).at[high], blocks.at[n - 1, high])
        return (
            remote(*to_right, send.at[s, 0], recv.at[s, 0], mp=right),
            remote(*to_left, send.at[s, 1], recv.at[s, 1], mp=left_dev),
        )

    q_copies = [gather_copies(s, q_ref, q_all, share // 2, q_send, q_recv) for s in range(half_n)]
    for copy in q_copies[0]:
        copy.start()

    part[...] = jnp.zeros_like(part)
    for block in range(n):
        if block % 2 == 1:
            s = block // 2
            for copy in q_copies[s]:
                copy.wait_recv()
            if s + 1 < half_n:
                for copy in q_copies[s + 1]:
                    copy.start()
        q_block = q_ref if block == 0 else q_all.at[block]
        for h in range(2):
            item = 2 * block + h
            for copy in loads(item):
                copy.wait()

            @pl.loop(0, half_rows // chunk if half_rows >= chunk else 1)
            def _(c, block=block, h=h, q_block=q_block):
                size = min(chunk, half_rows)
                at = pl.ds(pl.multiple_of(c * size, 16), size)
                blended = mom_st[h, at, :] + grad_st[h, at, :].astype(f32)
                high, low = split(blended)
                to = pl.ds(pl.multiple_of(h * half_rows + c * size, 16), size)
                b_high[block, to, :] = high
                b_low[block, to, :] = low
                q = q_block[...]
                part[to, :] += jnp.dot(high, q, preferred_element_type=f32) + jnp.dot(
                    low, q, preferred_element_type=f32
                )

            if item + 2 < 2 * n:
                for copy in loads(item + 2):
                    copy.start()

    core = lax.rem(my_dp, 2)
    mate = my_dp + 1 - 2 * core

    def rows_of(which):
        return pl.ds(pl.multiple_of(which * half_rows, 16), half_rows)

    mine = rows_of(core)
    dp_copies = [remote(part.at[rows_of(1 - core)], part_in.at[0], dp_send.at[0], dp_recv.at[0], dp=mate)]
    dp_copies[0].start()
    dp_copies[0].wait_recv()
    part[mine, :] += part_in[0]
    for t in range(1, n_dp // 2):
        copy = remote(part.at[mine], part_in.at[t], dp_send.at[t], dp_recv.at[t], dp=dp_peer(2 * t))
        copy.start()
        dp_copies.append(copy)
    total = part[mine, :]
    for t in range(1, n_dp // 2):
        dp_copies[t].wait_recv()
        total = total + part_in[t]
    left[mine, :] = total
    handout = remote(left.at[mine], left.at[mine], dp_send.at[n_dp // 2], dp_recv.at[n_dp // 2], dp=mate)
    handout.start()
    handout.wait_recv()
    transposed = left[...].T
    left_t[...] = transposed
    high, low = split(transposed)
    left_cat[:rank, :] = high
    left_cat[rank:, :] = low

    def make_w(offset):
        k = slot(offset)
        b = b_high[k]
        both = jnp.dot(left_cat[...], b, preferred_element_type=f32)
        w[k] = both[:rank] + both[rank:] + jnp.dot(left_cat[:rank, :], b_low[k], preferred_element_type=f32)

    low_half, high_half = pl.ds(0, half_rank), pl.ds(half_rank, half_rank)

    def ring_copies(s):
        return (
            remote(w.at[slot(-1 - s), low_half], right_in.at[s], rs_send.at[s, 0], rs_recv.at[s, 0], mp=right),
            remote(w.at[slot(1 + s), high_half], left_in.at[s], rs_send.at[s, 1], rs_recv.at[s, 1], mp=left_dev),
        )

    def gram_copy(bit):
        return remote(gram.at[bit], gram_in.at[bit], gr_send.at[bit], gr_recv.at[bit], mp=partner(bit))

    lane = lax.broadcasted_iota(jnp.int32, (rank, rank), 1)
    line = lax.broadcasted_iota(jnp.int32, (rank, rank), 0)

    def eliminate(first, last):
        @pl.loop(first, last)
        def _(k):
            row = aug[pl.ds(k, 1), :]
            column = jnp.sum(jnp.where(lane == k, aug[:, :rank], 0.0), axis=1, keepdims=True)
            pivot = jnp.sum(jnp.where(lane[:1] == k, row[:, :rank], 0.0), axis=1, keepdims=True)
            factor = jnp.where(line[:, :1] > k, column / pivot, 0.0)
            aug[...] = aug[...] - factor * row

    spare = n - 1 - n_bits
    per_step = -(-rank // max(spare, 1))
    made = set()

    def make_once(offset):
        if slot(offset) not in made:
            made.add(slot(offset))
            make_w(offset)

    make_once(-1)
    make_once(1)
    copies = []
    for s in range(n - 1):
        if s > 0:
            before = copies[s - 1]
            before[0].wait_recv()
            k = slot(-1 - s)
            w[k, low_half, :] += right_in[s - 1]
            before[1].wait_recv()
            k = slot(1 + s)
            w[k, high_half, :] += left_in[s - 1]
        copies.append(ring_copies(s))
        for copy in copies[s]:
            copy.start()
        if s == 0:
            gram[0] = jnp.dot(left_t[...], left[...], precision=highest, preferred_element_type=f32)
            gram_copy(0).start()
        elif s <= n_bits:
            gram_copy(s - 1).wait_recv()
            gram[s] = gram[s - 1] + gram_in[s - 1]
            if s < n_bits:
                gram_copy(s).start()
        if s + 1 <= half_n:
            make_once(-2 - s)
            make_once(2 + s)
        if s == half_n - 1 or n == 2:
            make_once(0)
        if s == n_bits:
            aug[:, :rank] = gram[n_bits]
            aug[:, rank:] = jnp.where(lane == line, 1.0, 0.0)
        if s >= n_bits and (s - n_bits) * per_step < rank:
            eliminate((s - n_bits) * per_step, min(rank, (s - n_bits + 1) * per_step))
    diagonal = jnp.sum(jnp.where(lane == line, aug[:, :rank], 0.0), axis=1, keepdims=True)
    inverse_low = aug[:, rank:] / jnp.sqrt(diagonal)

    copies[n - 2][0].wait_recv()
    w[0, low_half, :] += right_in[n - 2]
    copies[n - 2][1].wait_recv()
    w[0, high_half, :] += left_in[n - 2]

    own = jnp.dot(inverse_low, w[0], precision=highest, preferred_element_type=f32)
    pr[0] = own
    ag_copies = gather_copies(0, pr.at[0], pr, half_rank, ag_send, ag_recv)
    for copy in ag_copies:
        copy.start()

    def keep(k):
        return pltpu.make_async_copy(pr.at[k], (pr_own, pr_before, pr_after)[k], out_sem.at[k])

    keep(0).start()

    def cs_copy(bit):
        return remote(cs.at[bit], cs_in.at[bit], cs_send.at[bit], cs_recv.at[bit], mp=partner(bit))

    def csd_copy(t):
        return remote(cs.at[n_bits], csd_in.at[t - 1], cs_send.at[n_bits + t - 1], cs_recv.at[n_bits + t - 1], dp=dp_peer(t))

    cs[0] = lax.dot_general(
        jnp.ones((8, share), f32), own * own, (((1,), (1,)), ((), ())), precision=highest, preferred_element_type=f32
    )
    cs_copy(0).start()
    ortho = lax.dot_general(
        left[...], inverse_low, (((1,), (1,)), ((), ())), precision=highest, preferred_element_type=f32
    )
    for bit in range(n_bits):
        cs_copy(bit).wait_recv()
        cs[bit + 1] = cs[bit] + cs_in[bit]
        if bit + 1 < n_bits:
            cs_copy(bit + 1).start()
    for t in range(1, n_dp):
        csd_copy(t).start()
    sums = cs[n_bits]
    for t in range(1, n_dp):
        csd_copy(t).wait_recv()
    for t in range(n_dp - 1):
        sums = sums + csd_in[t]
    scale = 1.0 / jnp.sqrt(sums[:1] + 1e-06)
    o_high, o_low = split(ortho * (scale_factor * scale))
    o_ref[:, :rank] = o_high
    o_ref[:, rank : 2 * rank] = o_low
    o_ref[:, 2 * rank :] = (feedback_rate * ortho).astype(bf16)
    qout_ref[...] = (pr[0].T * scale).astype(bf16)
    for copy, k in zip(ag_copies, (1, 2)):
        copy.wait_recv()
        keep(k).start()

    for group in (q_copies, [ag_copies], copies):
        for pair_of in group:
            for copy in pair_of:
                copy.wait_send()
    for copy in dp_copies + [handout]:
        copy.wait_send()
    for bit in range(n_bits):
        gram_copy(bit).wait_send()
        cs_copy(bit).wait_send()
    for t in range(1, n_dp):
        csd_copy(t).wait_send()
    for k in range(3):
        keep(k).wait()


def outputs_kernel(pieces, idx_ref, mom_ref, grad_ref, o_ref, *refs):
    del idx_ref
    block = pl.program_id(0)
    mom_out, update_out, twice, low_part = refs[-4:]
    rank = low_part.shape[0]

    @pl.when(pl.program_id(1) == 0)
    def _():
        values, first = [], 0
        for count in pieces:
            parts = [ref[...] for ref in refs[first : first + count]]
            values.append(parts[0] if count == 1 else jnp.concatenate(parts, axis=0))
            first += count
        value = values[0]
        for k in range(1, len(values)):
            value = jnp.where(block == k, values[k], value)
        high, low = split(value)
        twice[:rank, :] = high
        twice[rank:, :] = high
        low_part[...] = low

    product = jnp.dot(o_ref[:, : 2 * rank], twice[...], preferred_element_type=f32)
    product += jnp.dot(o_ref[:, :rank], low_part[...], preferred_element_type=f32)
    update_out[...] = product.astype(bf16)
    blended = mom_ref[...] + grad_ref[...].astype(f32)
    mom_out[...] = blended - jnp.dot(o_ref[:, 2 * rank :], twice[:rank, :], preferred_element_type=f32)


def write_outputs(blocks, owners, momentum, gradient, ortho, outputs):
    rows, cols = momentum.shape
    pieces = tuple(len(parts) for parts in blocks)
    flat = [part for parts in blocks for part in parts]
    share = flat[0].shape[1]
    rank = ortho.shape[1] // 3
    tile = rows // 2
    def columns():
        return pl.BlockSpec((tile, share), lambda j, i, idx: (i, idx[j]))

    whole = pl.BlockSpec(memory_space=pltpu.VMEM)
    anywhere = pl.BlockSpec(memory_space=pl.ANY)
    given = [] if outputs is None else list(outputs)
    kernel = functools.partial(outputs_kernel, pieces)
    first = 4 + len(flat)
    area = len(blocks) * rows * share
    return pl.pallas_call(
        kernel,
        grid_spec=pltpu.PrefetchScalarGridSpec(
            num_scalar_prefetch=1,
            grid=(len(blocks), rows // tile),
            in_specs=[
                columns(),
                columns(),
                pl.BlockSpec((tile, 3 * rank), lambda j, i, idx: (i, 0)),
                *[whole for _ in flat],
                *[anywhere for _ in given],
            ],
            out_specs=(columns(), columns()),
            scratch_shapes=[pltpu.VMEM((2 * rank, share), bf16), pltpu.VMEM((rank, share), bf16)],
        ),
        out_shape=(
            jax.ShapeDtypeStruct((rows, cols), f32),
            jax.ShapeDtypeStruct((rows, cols), bf16),
        ),
        input_output_aliases={first: 0, first + 1: 1} if given else {},
        cost_estimate=pl.CostEstimate(flops=8 * rank * area, bytes_accessed=12 * area, transcendentals=0),
        compiler_params=pltpu.CompilerParams(vmem_limit_bytes=60 * 1024 * 1024),
    )(owners, momentum, gradient, ortho, *flat, *given)


def fused(n, n_dp, scale_factor, momentum, gradient, factor_q):
    rows, cols = momentum.shape
    share, rank = factor_q.shape
    n_bits = n.bit_length() - 1
    half_n = n // 2
    dma = pltpu.SemaphoreType.DMA
    vmem = pltpu.VMEM
    whole = pl.BlockSpec(memory_space=pltpu.VMEM)
    anywhere = pl.BlockSpec(memory_space=pl.ANY)
    own, before, after, ortho, q_new = pl.pallas_call(
        functools.partial(factors_kernel, n, n_dp, scale_factor),
        out_shape=(
            *[jax.ShapeDtypeStruct((rank, share), f32)] * 3,
            jax.ShapeDtypeStruct((rows, 3 * rank), bf16),
            jax.ShapeDtypeStruct((share, rank), bf16),
        ),
        in_specs=[anywhere, anywhere, whole],
        out_specs=(anywhere, anywhere, anywhere, whole, whole),
        scratch_shapes=[
            vmem((n, rows, share), bf16),
            vmem((n, rows, share), bf16),
            vmem((n, share, rank), bf16),
            vmem((2, rows // 2, share), f32),
            vmem((2, rows // 2, share), bf16),
            vmem((rows, rank), f32),
            vmem((n_dp // 2, rows // 2, rank), f32),
            vmem((rows, rank), f32),
            vmem((rank, rows), f32),
            vmem((2 * rank, rows), bf16),
            vmem((n, rank, share), f32),
            vmem((n - 1, rank // 2, share), f32),
            vmem((n - 1, rank // 2, share), f32),
            vmem((n_bits + 1, rank, rank), f32),
            vmem((n_bits, rank, rank), f32),
            vmem((rank, 2 * rank), f32),
            vmem((3, rank, share), f32),
            vmem((n_bits + 1, 8, rank), f32),
            vmem((n_bits, 8, rank), f32),
            vmem((n_dp - 1, 8, rank), f32),
            dma((2, 2)),
            dma((half_n, 2)),
            dma((half_n, 2)),
            dma((n_dp // 2 + 1,)),
            dma((n_dp // 2 + 1,)),
            dma((n - 1, 2)),
            dma((n - 1, 2)),
            dma((n_bits,)),
            dma((n_bits,)),
            dma((1, 2)),
            dma((1, 2)),
            dma((n_bits + n_dp - 1,)),
            dma((n_bits + n_dp - 1,)),
            dma((3,)),
        ],
        compiler_params=pltpu.CompilerParams(
            collective_id=0, has_side_effects=True, vmem_limit_bytes=60 * 1024 * 1024
        ),
    )(momentum, gradient, factor_q)

    ring = [2 * p if p < half_n else 2 * (n - 1 - p) + 1 for p in range(n)]
    up = [(ring[p], ring[(p + 1) % n]) for p in range(n)]
    down = [(b, a) for a, b in up]
    me = lax.axis_index("mp")
    odd = lax.rem(me, 2)
    place = (1 - odd) * lax.div(me, 2) + odd * (n - 1 - lax.div(me, 2))

    def owners(*offsets):
        at = lax.rem(place + n + jnp.array(offsets, jnp.int32), jnp.int32(n))
        back = lax.div(at, jnp.int32(half_n))
        return (1 - back) * (2 * at) + back * (2 * (n - 1 - at) + 1)

    outputs = None
    ready, at = [(own,), (before,), (after,)], owners(0, -1, 1)
    for s in range(1, half_n):
        if s < half_n - 1:
            before = lax.ppermute(before, "mp", up)
            after = lax.ppermute(after, "mp", down)
            coming, then = [(before,), (after,)], owners(-1 - s, 1 + s)
        else:
            low = lax.ppermute(before[: rank // 2], "mp", up)
            high = lax.ppermute(after[rank // 2 :], "mp", down)
            coming, then = [(low, high)], owners(half_n)
        outputs = write_outputs(ready, at, momentum, gradient, ortho, outputs)
        outputs, coming = lax.optimization_barrier((outputs, coming))
        if s < half_n - 1:
            (before,), (after,) = coming
        ready, at = coming, then
    momentum_out, update = write_outputs(ready, at, momentum, gradient, ortho, outputs)
    return momentum_out, q_new, update


def solution(mesh):
    n, n_dp = mesh.shape["mp"], mesh.shape["dp"]

    def local(momentum, gradient, factor_q):
        rows, cols = momentum.shape
        share, rank = factor_q.shape
        scale_factor = math.sqrt(rows * n * cols * n_dp / rank)
        tiles = (
            share % 128 == 0
            and rank % 128 == 0
            and rows % (32 * n_dp) == 0
            and n >= 4
            and n & (n - 1) == 0
            and n_dp % 2 == 0
            and 4 * rows * cols <= 32 * 1024 * 1024
        )
        if tiles:
            return fused(n, n_dp, scale_factor, momentum, gradient, factor_q)
        return plain(scale_factor, momentum, gradient, factor_q)

    return jax.shard_map(
        local,
        mesh=mesh,
        in_specs=(P("mp", "dp"), P("mp", "dp"), P(("dp", "mp"), None)),
        out_specs=(P("mp", "dp"), P(("dp", "mp"), None), P("mp", "dp")),
        check_vma=False,
    )
```
